512 devices in a mesh: src: 32 (over y, x), tgt: 16 (over z, core).
Axes of the slice: x: 4, y: 8, z: 8, core: 2. Of those that a mesh axis runs over, the one named last changes fastest.
Arguments:
- features: bfloat16 [65536, 128], P(('tgt', 'src')), may hold values from -8 to 8
- adjacency: bfloat16 [16, 32, 128, 128, 128], P('tgt', 'src'), may hold values from 0 to 600, as said below
- tile_slot: int32 [16, 32, 128], P('tgt', 'src'), may hold values from 0 to 511, as said below
- tile_live: int32 [16, 32, 128], P('tgt', 'src'), may hold values from 0 to 1, as said below
- first_weight: bfloat16 [128, 256], replicated, may hold values from -0.5 to 0.5
- second_weight: bfloat16 [256, 256], replicated, may hold values from -0.375 to 0.375
Outputs:
- embedding: bfloat16 [65536, 256], P(('tgt', 'src'))
The draws below stay inside these ranges and needn't reach their ends.
Inputs may be any that keep to these rules, and one draw needn't show every extreme that they name: `adjacency`: nonnegative edge weights; on average about min(0.3, 4 / 128) of a tile's entries are nonzero. `tile_slot`: a slot's value is local target block * 16 + local source block. `tile_live`: on each device the live slots come first; each device has 32 to 128 live slots, and some device has all 128 live.
All inputs are finite; a program needn't handle non-finite values.
Results may differ from the reference program's by a relative error of at most 0.023.
Values may be sent and summed in bfloat16 or wider, within the bound.
A program may use at most 64 MiB of HBM per device.

```python
import math
import jax
import jax.numpy as jnp
from jax import lax

IN_F = 128
HID = 256
BLOCK = 128
ROWS_DEV = 128
TILES_DEV = 128
NODES = 65536
TGT_BLOCKS = 32
SRC_BLOCKS = 16
N_SRC = 32
N_TGT = 16


def common_slots(key):
    slot_key = jax.random.fold_in(key, 101)
    return jax.random.randint(slot_key, (N_TGT, N_SRC, TILES_DEV), 0, TGT_BLOCKS * SRC_BLOCKS).astype(jnp.int32)


def draw_tile_slot(key, part):
    return common_slots(key)


def draw_features(key, part):
    key = jax.random.fold_in(key, 13)
    first = jax.random.fold_in(key, 0)
    noise = jax.random.normal(first, (NODES, IN_F), jnp.float32)
    return jnp.clip(noise, -6.0, 6.0).astype(jnp.bfloat16)


def draw_adjacency(key, part):
    slots = common_slots(key)
    key = jax.random.fold_in(key, 7)
    first = jax.random.fold_in(key, 0)
    second = jax.random.fold_in(key, 1)
    fourth = jax.random.fold_in(key, 3)
    shape = (N_TGT, N_SRC, TILES_DEV, BLOCK, BLOCK)
    per_block = ROWS_DEV // BLOCK
    node_factor = jnp.exp(jax.random.uniform(fourth, (NODES // BLOCK, BLOCK), jnp.float32, math.log(0.001), 0.0))
    group_index = jnp.arange(N_TGT, dtype=jnp.int32).reshape(N_TGT, 1, 1)
    source_index = jnp.arange(N_SRC, dtype=jnp.int32).reshape(1, N_SRC, 1)
    local_target = slots // SRC_BLOCKS
    local_source = slots % SRC_BLOCKS
    target_block = group_index * TGT_BLOCKS + local_target
    source_block = (local_source // per_block * N_SRC + source_index) * per_block + local_source % per_block
    row_scale = node_factor[target_block]
    column_scale = node_factor[source_block]
    heavy_source = jax.random.randint(jax.random.fold_in(key, 21), (N_TGT, 1, 1), 0, N_SRC)
    heavy_peer = jax.random.randint(jax.random.fold_in(key, 22), (N_TGT, N_SRC, 1), 0, N_TGT)
    source_peer = local_source // per_block
    emphasis = jnp.where(source_index == heavy_source, 10.0, 1.0) * jnp.where(source_peer == heavy_peer, 10.0, 1.0)
    density = min(0.3, 4.0 / BLOCK)
    present = jax.random.bernoulli(first, density, shape).astype(jnp.float32)
    position = jnp.arange(N_SRC, dtype=jnp.float32).reshape(1, N_SRC, 1, 1, 1)
    rising = 1.0 + 2.0 * position / max(N_SRC - 1, 1)
    values = jax.random.uniform(second, shape, jnp.float32, 0.5, 1.5)
    values = values * row_scale[:, :, :, :, None] * column_scale[:, :, :, None, :]
    values = values * emphasis[:, :, :, None, None]
    return (present * values * rising).astype(jnp.bfloat16)


def draw_tile_live(key, part):
    key = jax.random.fold_in(key, 11)
    first, second = jax.random.split(key)
    counts = jax.random.randint(first, (N_TGT * N_SRC,), TILES_DEV // 4, TILES_DEV + 1)
    chosen = jax.random.randint(second, (), 0, N_TGT * N_SRC)
    counts = jnp.where(jnp.arange(N_TGT * N_SRC) == chosen, TILES_DEV, counts)
    slots = jnp.arange(TILES_DEV)
    live = (slots[None, :] < counts[:, None]).astype(jnp.int32)
    return live.reshape(N_TGT, N_SRC, TILES_DEV)


def normal_values(rng, dims, scale, limit, held_as=jnp.bfloat16):
    result = jax.random.normal(rng, dims, jnp.float32) * scale
    return jnp.minimum(jnp.maximum(result, -limit), limit).astype(held_as)


def setup_inputs(seed: int = 0) -> dict:
    splits = jax.random.split(jax.random.key(seed), 7)
    return {
        "features": draw_features(jax.random.fold_in(splits[6], 71), 0),
        "adjacency": draw_adjacency(jax.random.fold_in(splits[6], 71), 0),
        "tile_slot": draw_tile_slot(jax.random.fold_in(splits[6], 71), 0),
        "tile_live": draw_tile_live(jax.random.fold_in(splits[6], 71), 0),
        "first_weight": normal_values(splits[4], (IN_F, HID), IN_F ** -0.5, 0.5),
        "second_weight": normal_values(splits[5], (HID, HID), HID ** -0.5, 0.375),
    }


def place_blocks(slot_index, target_group, source_group):
    per_block = ROWS_DEV // BLOCK
    local_target = slot_index // SRC_BLOCKS
    local_source = slot_index % SRC_BLOCKS
    target_block = target_group * TGT_BLOCKS + local_target
    source_block = (local_source // per_block * N_SRC + source_group) * per_block + local_source % per_block
    return (local_target.astype(jnp.int32), target_block.astype(jnp.int32), source_block.astype(jnp.int32))

def reference(features, adjacency, tile_slot, tile_live, first_weight, second_weight):
    devices = N_TGT * N_SRC
    all_blocks = NODES // BLOCK
    tile_stack = adjacency.reshape(devices, TILES_DEV, BLOCK, BLOCK)
    slot_stack = tile_slot.reshape(devices, TILES_DEV)
    live_stack = tile_live.reshape(devices, TILES_DEV).astype(jnp.float32)
    numbers = jnp.arange(devices, dtype=jnp.int32)

    def degree_step(accumulated, element):
        number, block_tiles, slot_index, slot_live = element
        local_target, target_block, source_block = place_blocks(slot_index, number // N_SRC, number % N_SRC)
        row_totals = lax.optimization_barrier(jnp.sum(block_tiles.astype(jnp.float32), axis=2)) * slot_live[:, None]
        return (accumulated.at[target_block].add(row_totals), None)
    degree, _ = lax.scan(degree_step, jnp.zeros((all_blocks, BLOCK), jnp.float32), (numbers, tile_stack, slot_stack, live_stack))
    inverse_root = lax.rsqrt(1.0 + degree.reshape(NODES))

    def convolve(hidden, weight):
        feature_width = hidden.shape[1]
        scaled = (inverse_root[:, None] * hidden.astype(jnp.float32)).astype(jnp.bfloat16)
        scaled_blocks = scaled.reshape(all_blocks, BLOCK, feature_width)

        def spread_step(accumulated, element):
            number, block_tiles, slot_index, slot_live = element
            target_group = number // N_SRC
            local_target, target_block, source_block = place_blocks(slot_index, target_group, number % N_SRC)
            sources = scaled_blocks[source_block].astype(jnp.float32)
            products = jnp.einsum('tij,tjf->tif', block_tiles.astype(jnp.float32), sources) * slot_live[:, None, None]
            partial_value = jnp.zeros((TGT_BLOCKS, BLOCK, feature_width), jnp.float32).at[local_target].add(products)
            rounded = lax.optimization_barrier(partial_value.astype(jnp.bfloat16))
            partial_value = rounded.astype(jnp.float32)
            offset = (target_group * TGT_BLOCKS).astype(jnp.int32)
            current = lax.dynamic_slice_in_dim(accumulated, offset, TGT_BLOCKS, 0)
            return (lax.dynamic_update_slice_in_dim(accumulated, current + partial_value, offset, 0), None)
        summed, _ = lax.scan(spread_step, jnp.zeros((all_blocks, BLOCK, feature_width), jnp.float32), (numbers, tile_stack, slot_stack, live_stack))
        summed = summed.reshape(NODES, feature_width)
        combined = (inverse_root[:, None] * (summed + scaled.astype(jnp.float32))).astype(jnp.bfloat16)
        return jax.nn.relu(jnp.dot(combined, weight, preferred_element_type=jnp.float32)).astype(jnp.bfloat16)
    hidden = convolve(features, first_weight)
    return convolve(hidden, second_weight)
```

```python
import functools

import jax
import jax.numpy as jnp
from jax import lax
from jax.experimental import pallas as pl
from jax.experimental.pallas import tpu as pltpu
from jax.sharding import PartitionSpec as P

MESH = pl.DeviceIdType.MESH
F32 = jnp.float32
BF16 = jnp.bfloat16
NX = 4
B = 128
H = B // 2
LOADS = 4


def wrap(a, n):
    return lax.rem(a + n, n)


def plan(nx, ny, nz, width1, width2):
    ns = 2 * nz
    rows = [
        ("dx_send", (nx, ny, B), F32),
        ("dx_recv", (nx, ny, B), F32),
        ("dy_send", (ny, 8, B), F32),
        ("dy_recv", (ny, 8, B), F32),
        ("roots", (ns, 8, B), F32),
        ("src1", (ns, B, width1), BF16),
        ("src2", (ns, B, width2), BF16),
    ]
    for layer, width in ((1, width1), (2, width2)):
        for chain, (n1, n2) in (("a", (ny, nx)), ("b", (nx, ny))):
            for way, steps in ((0, n1 // 2), (1, (n1 - 1) // 2)):
                for end in ("send", "recv"):
                    rows.append((f"{chain}1{way}{layer}{end}", (max(steps, 1), n2, H, width), BF16))
            for way, steps in ((0, n2 // 2), (1, (n2 - 1) // 2)):
                for end in ("send", "recv"):
                    rows.append((f"{chain}2{way}{layer}{end}", (max(steps, 1), H, width), BF16))
    return rows


class Links:
    def __init__(self, send_sems, recv_sems):
        self.send_sems, self.recv_sems = send_sems, recv_sems
        self.count = 0
        self.sent = []

    def copy(self, src, dst, device):
        number = self.count
        self.count += 1
        made = pltpu.make_async_remote_copy(
            src_ref=src,
            dst_ref=dst,
            send_sem=self.send_sems.at[number],
            recv_sem=self.recv_sems.at[number],
            device_id=device,
            device_id_type=MESH,
        )
        made.start()
        self.sent.append(made)
        return made

    def finish(self):
        for made in self.sent:
            made.wait_send()


def order(slot, live, nb, count):
    lane = lax.broadcasted_iota(jnp.int32, (B, B), 1)
    sub = lax.broadcasted_iota(jnp.int32, (B, B), 0)
    value = jnp.broadcast_to(jnp.where(live > 0, slot, nb), (B, B))
    value_t = value.T
    key, key_t = value * count + lane, value_t * count + sub
    rank = jnp.sum((key_t < key).astype(jnp.int32), axis=0, keepdims=True)
    chosen = (jnp.broadcast_to(rank, (B, B)).T == lane).astype(jnp.int32)
    rows = [
        jnp.sum(chosen * sub, axis=0, keepdims=True),
        jnp.sum(chosen * value_t, axis=0, keepdims=True),
    ]
    for j in range(-(-nb // B)):
        block = lane + j * B
        upto = jnp.sum((value_t <= block).astype(jnp.int32), axis=0, keepdims=True)
        below = jnp.sum((value_t < block).astype(jnp.int32), axis=0, keepdims=True)
        rows.append(jnp.where(upto > below, upto - 1, count))
    while len(rows) < 8:
        rows.append(jnp.zeros((1, B), jnp.int32))
    return value, jnp.concatenate(rows, axis=0)


def kernel(dims, names, feat, adj, slot, live, w1, w2, out, *scratch):
    nx, ny, nz = dims
    nt, ns = nx * ny, 2 * nz
    nb = nt * ns
    count = adj.shape[0]
    buf = dict(zip(names, scratch))
    (tiles, sums, rowsum, dense_a, dense_b, acc_a0, acc_a1, acc_a2, acc_b0, acc_b1, acc_b2,
     ready1, scaled1, index_v, index_s, load_sems, index_sem, send_sems, recv_sems) = scratch[len(names):]
    accs_a, accs_b = (acc_a0, acc_a1, acc_a2), (acc_b0, acc_b1, acc_b2)
    links = Links(send_sems, recv_sems)

    me_s, me_t = lax.axis_index("src"), lax.axis_index("tgt")
    y, x = me_s // nx, lax.rem(me_s, nx)
    z, core = me_t // 2, lax.rem(me_t, 2)
    sign = 1 - 2 * core

    def at_x(d):
        return {"src": y * nx + wrap(x + d, nx)}

    def at_y(d):
        return {"src": wrap(y + d, ny) * nx + x}

    def at_z(d):
        return {"tgt": wrap(z + d, nz) * 2 + core}

    sibling = {"tgt": z * 2 + 1 - core}

    per_load = count // LOADS
    loads = []
    for j in range(LOADS):
        part = pl.ds(j * per_load, per_load)
        loads.append(pltpu.make_async_copy(adj.at[part], tiles.at[part], load_sems.at[j]))
        loads[-1].start()
    barrier = pltpu.get_barrier_semaphore()
    greeted = 0
    for d in range(1, nx):
        pl.semaphore_signal(barrier, inc=1, device_id=at_x(d), device_id_type=MESH)
        greeted += 1
    for d in range(1, ny):
        pl.semaphore_signal(barrier, inc=1, device_id=at_y(d), device_id_type=MESH)
        greeted += 1
    for d in range(1, ns):
        pl.semaphore_signal(
            barrier, inc=1, device_id={"tgt": lax.rem(me_t + d, ns)}, device_id_type=MESH
        )
        greeted += 1

    value, found = order(slot[...], live[...], nb, count)
    index_v[...] = found
    to_smem = pltpu.make_async_copy(index_v, index_s, index_sem)
    to_smem.start()

    buf["src1"][me_t] = feat[...]
    pl.semaphore_wait(barrier, greeted)

    def gather_start(ref, first, size):
        part = pl.ds(first, size)
        state = {"ref": ref, "part": part, "long": [], "short": [], "sibling": []}
        mine = ref.at[me_t, part]
        state["sibling"].append(links.copy(mine, mine, sibling))
        if nz > 1:
            state["long"].append(links.copy(mine, mine, at_z(sign)))
        if (nz - 1) // 2:
            state["short"].append(links.copy(mine, mine, at_z(-sign)))
        return state

    def gather_step(state, k):
        ref = state["ref"]
        for way, steps, d in (("long", nz // 2, sign), ("short", (nz - 1) // 2, -sign)):
            if k < steps:
                state[way][k].wait_recv()
                got = ref.at[wrap(z - d * (k + 1), nz) * 2 + core, state["part"]]
                if k + 1 < steps:
                    state[way].append(links.copy(got, got, at_z(d)))
                state["sibling"].append(links.copy(got, got, sibling))

    def gather_finish(state):
        for made in state["sibling"]:
            made.wait_recv()

    gathered = gather_start(buf["src1"], 0, B)

    ones = jnp.ones((8, B), BF16)
    group = min(16, per_load)
    for j in range(LOADS):
        loads[j].wait()

        def sum_rows(i, carry, j=j):
            first = j * per_load + i * group
            part = tiles[pl.ds(first, group)].reshape(group * B, B)
            got = lax.dot_general(ones, part, (((1,), (1,)), ((), ())), preferred_element_type=F32)
            for q in range(group):
                rowsum[first // group, q : q + 1, :] = got[0:1, q * B : (q + 1) * B]
            return carry

        lax.fori_loop(0, per_load // group, sum_rows, 0)
    row = lax.broadcasted_iota(jnp.int32, (nt, B), 0)
    target = lax.rem(row, ny) * nx + row // ny
    value_row = value[0:1]
    mine = (value_row >= target * ns) & (value_row < (target + 1) * ns)
    degree = jnp.dot(
        mine.astype(F32),
        rowsum[...].reshape(count, B),
        preferred_element_type=F32,
        precision=lax.Precision.HIGHEST,
    )
    for i in range(nx):
        buf["dx_send"][i] = degree[i * ny : (i + 1) * ny]
    dx = [
        links.copy(buf["dx_send"].at[wrap(x + d, nx)], buf["dx_recv"].at[d], at_x(d))
        for d in range(1, nx)
    ]

    to_smem.wait()
    sums[count] = jnp.zeros((B, B), BF16)

    def add_tile(i, carry):
        before, total = carry
        now = index_s[1, i]
        same = jnp.where(now == before, 1.0, 0.0).astype(F32)
        total = tiles[jnp.clip(index_s[0, i], 0, count - 1)].astype(F32) + total * same
        sums[i] = total.astype(BF16)
        return now, total

    lax.fori_loop(0, count, add_tile, (jnp.int32(-1), jnp.zeros((B, B), F32)), unroll=2)

    for made in dx:
        made.wait_recv()
    part = buf["dx_send"][x]
    for d in range(1, nx):
        part = part + buf["dx_recv"][d]
    for i in range(ny):
        buf["dy_send"][i] = jnp.broadcast_to(part[i : i + 1], (8, B))
    dy = [
        links.copy(buf["dy_send"].at[wrap(y + d, ny)], buf["dy_recv"].at[d], at_y(d))
        for d in range(1, ny)
    ]
    gather_step(gathered, 0)

    def place(t, carry):
        ty, tx = t // nx, lax.rem(t, nx)
        for c in range(ns):
            v = t * ns + c
            tile = sums[jnp.clip(index_s[2 + v // B, lax.rem(v, B)], 0, count)]
            dense_a[ty, tx, :, c * B : (c + 1) * B] = tile[:H]
            dense_b[tx, ty, :, c * B : (c + 1) * B] = tile[H:]
        return carry

    lax.fori_loop(0, nt // 2, place, 0)
    for made in dy:
        made.wait_recv()
    total = buf["dy_send"][y] + 1.0
    for d in range(1, ny):
        total = total + buf["dy_recv"][d]
    root = lax.rsqrt(total)
    buf["roots"][me_t] = root
    exchanged = [
        links.copy(
            buf["roots"].at[me_t], buf["roots"].at[me_t], {"tgt": lax.rem(me_t + d, ns)}
        )
        for d in range(1, ns)
    ]
    gather_step(gathered, 1)
    lax.fori_loop(nt // 2, nt, place, 0)
    for k in range(2, nz // 2):
        gather_step(gathered, k)
    own_root = jnp.broadcast_to(root[0:1], (B, B)).T
    scaled1[...] = (own_root * feat[...].astype(F32)).astype(BF16)
    gather_finish(gathered)
    for made in exchanged:
        made.wait_recv()
    roots_t = buf["roots"][...].reshape(ns * 8, B).T
    for c in range(ns):
        ready1[c] = (roots_t[:, 8 * c : 8 * c + 1] * buf["src1"][c].astype(F32)).astype(BF16)

    def spread(layer, width):
        source = ready1 if layer == 1 else buf["src2"]
        blocks = min(4, ns)

        def product(panel, acc, n2):
            def step(k, carry):
                left = panel[:, :, pl.ds(pl.multiple_of(k * blocks * B, B), blocks * B)]
                right = source[pl.ds(k * blocks, blocks)].reshape(blocks * B, width)
                got = jnp.dot(left.reshape(n2 * H, blocks * B), right, preferred_element_type=F32)
                got = got.reshape(n2, H, width)

                @pl.when(k == 0)
                def _():
                    acc[:, :, 0:width] = got

                @pl.when(k > 0)
                def _():
                    acc[:, :, 0:width] += got

                return carry

            lax.fori_loop(0, ns // blocks, step, 0)

        class Chain:
            def __init__(self, name, dense, accs, n1, n2, p1, p2, at1, at2):
                self.name, self.dense, self.accs = name, dense, accs
                self.n1, self.n2, self.p1, self.p2, self.at1, self.at2 = n1, n2, p1, p2, at1, at2
                self.steps1 = (n1 // 2, (n1 - 1) // 2)
                self.steps2 = (n2 // 2, (n2 - 1) // 2)
                self.made1, self.made2 = ({}, {}), ({}, {})
                self.size = 2 if n2 % 2 == 0 else 1
                self.subs = n2 // self.size

            def refs(self, phase, way):
                key = f"{self.name}{phase}{way}{layer}"
                return buf[key + "send"], buf[key + "recv"]

            def multiply(self, way, k):
                d = sign if way == 0 else -sign
                place = wrap(self.p1 + d * (self.steps1[way] - k), self.n1)
                product(self.dense.at[place], self.accs[way], self.n2)

            def multiply_own(self):
                product(self.dense.at[self.p1], self.accs[2], self.n2)

            def send1(self, way, k, j):
                d = sign if way == 0 else -sign
                send, recv = self.refs(1, way)
                at = pl.ds(j * self.size, self.size)
                value = self.accs[way][at, :, 0:width]
                if k:
                    self.made1[way][k - 1, j].wait_recv()
                    value = value + recv[k - 1, at].astype(F32)
                send[k, at] = value.astype(BF16)
                self.made1[way][k, j] = links.copy(send.at[k, at], recv.at[k, at], self.at1(d))

            def middle(self, j):
                at = pl.ds(j * self.size, self.size)
                value = self.accs[2][at, :, 0:width]
                for way, steps in enumerate(self.steps1):
                    if steps:
                        self.made1[way][steps - 1, j].wait_recv()
                        value = value + self.refs(1, way)[1][steps - 1, at].astype(F32)
                self.accs[2][at, :, 0:width] = value

            def send2(self, way, k):
                d = sign if way == 0 else -sign
                send, recv = self.refs(2, way)
                value = self.accs[2][wrap(self.p2 + d * (self.steps2[way] - k), self.n2), :, 0:width]
                if k:
                    self.made2[way][k - 1].wait_recv()
                    value = value + recv[k - 1].astype(F32)
                send[k] = value.astype(BF16)
                self.made2[way][k] = links.copy(send.at[k], recv.at[k], self.at2(d))

            def end(self):
                value = self.accs[2][self.p2, :, 0:width]
                for way, steps in enumerate(self.steps2):
                    if steps:
                        self.made2[way][steps - 1].wait_recv()
                        value = value + self.refs(2, way)[1][steps - 1].astype(F32)
                return value

            def events(self, unit, shift):
                found = []
                for way, steps in enumerate(self.steps1):
                    for k in range(steps):
                        before = (k - 1) * unit + 0.5 * unit / self.subs if k else -1.0
                        found.append((before + shift + 0.1 * way, functools.partial(self.multiply, way, k)))
                        for j in range(self.subs):
                            at = (k - 1) * unit + unit * (j + 1) / self.subs if k else -1.0
                            found.append((at + shift + 0.1 * way, functools.partial(self.send1, way, k, j)))
                last = max(self.steps1) * unit
                found.append((last - unit + 0.5 * unit / self.subs + shift, self.multiply_own))
                for j in range(self.subs):
                    found.append((last - unit + unit * (j + 1) / self.subs + shift, functools.partial(self.middle, j)))
                for way, steps in enumerate(self.steps2):
                    for k in range(steps):
                        at = last + 0.01 + 0.8 * k
                        found.append((at + shift + 0.1 * way, functools.partial(self.send2, way, k)))
                return found

        a = Chain("a", dense_a, accs_a, ny, nx, y, x, at_y, at_x)
        b = Chain("b", dense_b, accs_b, nx, ny, x, y, at_x, at_y)
        events = a.events(1.0, 0.0) + b.events(a.steps1[0] / max(b.steps1[0], 1), 0.05)
        for _, event in sorted(events, key=lambda entry: entry[0]):
            event()
        return a.end, b.end

    def finish_rows(end, first, scaled, weight):
        summed = end()
        root_b = jnp.concatenate([own_root[first : first + H]] * (summed.shape[1] // B), axis=1)
        combined = (root_b * (summed + scaled.astype(F32))).astype(BF16)
        got = jnp.dot(combined, weight[...], preferred_element_type=F32)
        return jnp.maximum(got, 0.0).astype(BF16)

    width1, width2 = feat.shape[1], w1.shape[1]
    gathers = []
    for half, end in enumerate(spread(1, width1)):
        rows = slice(half * H, (half + 1) * H)
        hidden = finish_rows(end, half * H, scaled1[rows], w1)
        root_2 = jnp.concatenate([own_root[rows]] * (width2 // B), axis=1)
        buf["src2"][me_t, rows] = (root_2 * hidden.astype(F32)).astype(BF16)
        gathers.append(gather_start(buf["src2"], half * H, H))
    for k in range(nz // 2):
        for state in gathers:
            gather_step(state, k)
    for state in gathers:
        gather_finish(state)
    for half, end in enumerate(spread(2, width2)):
        rows = slice(half * H, (half + 1) * H)
        out[rows] = finish_rows(end, half * H, buf["src2"][me_t, rows], w2)
    links.finish()


def on_device(dims, features, adjacency, tile_slot, tile_live, first_weight, second_weight):
    nx, ny, nz = dims
    nt, ns = nx * ny, 2 * nz
    count = adjacency.shape[2]
    width1, width2 = first_weight.shape
    rows = plan(nx, ny, nz, width1, width2)
    copies = 300
    vmem = pl.BlockSpec(memory_space=pltpu.VMEM)
    group = min(16, count // LOADS)
    return pl.pallas_call(
        functools.partial(kernel, dims, [name for name, _, _ in rows]),
        out_shape=jax.ShapeDtypeStruct((B, second_weight.shape[1]), BF16),
        in_specs=[vmem, pl.BlockSpec(memory_space=pl.ANY), vmem, vmem, vmem, vmem],
        out_specs=vmem,
        scratch_shapes=[pltpu.VMEM(shape, dtype) for _, shape, dtype in rows]
        + [
            pltpu.VMEM((count, B, B), BF16),
            pltpu.VMEM((count + 1, B, B), BF16),
            pltpu.VMEM((count // group, group, B), F32),
            pltpu.VMEM((ny, nx, H, ns * B), BF16),
            pltpu.VMEM((nx, ny, H, ns * B), BF16),
            *[pltpu.VMEM((nx, H, width2), F32)] * 3,
            *[pltpu.VMEM((ny, H, width2), F32)] * 3,
            pltpu.VMEM((ns, B, width1), BF16),
            pltpu.VMEM((B, width1), BF16),
            pltpu.VMEM((8, B), jnp.int32),
            pltpu.SMEM((8, B), jnp.int32),
            pltpu.SemaphoreType.DMA((LOADS,)),
            pltpu.SemaphoreType.DMA,
            pltpu.SemaphoreType.DMA((copies,)),
            pltpu.SemaphoreType.DMA((copies,)),
        ],
        compiler_params=pltpu.CompilerParams(
            collective_id=0, has_side_effects=True, vmem_limit_bytes=56 * 2**20
        ),
    )(
        features,
        adjacency[0, 0],
        tile_slot[0],
        tile_live[0],
        first_weight,
        second_weight,
    )


def solution(mesh, nx=NX):
    dims = (nx, mesh.shape["src"] // nx, mesh.shape["tgt"] // 2)
    placed = (
        P(("tgt", "src"), None),
        P("tgt", "src", None, None, None),
        P("tgt", "src", None),
        P("tgt", "src", None),
        P(),
        P(),
    )
    return jax.shard_map(
        functools.partial(on_device, dims),
        mesh=mesh,
        in_specs=placed,
        out_specs=P(("tgt", "src"), None),
        check_vma=False,
    )
```

```python
import functools

import jax
import jax.numpy as jnp
from jax import lax
from jax.experimental import pallas as pl
from jax.experimental.pallas import tpu as pltpu
from jax.sharding import PartitionSpec as P

MESH = pl.DeviceIdType.MESH
F32 = jnp.float32
BF16 = jnp.bfloat16
NX = 4
B = 128
H = B // 2
LOADS = 4


def wrap(a, n):
    return lax.rem(a + n, n)


def plan(nx, ny, nz, width1, width2):
    ns = 2 * nz
    rows = [
        ("dx_send", (nx, ny, B), F32),
        ("dx_recv", (nx, ny, B), F32),
        ("dy_send", (ny, 8, B), F32),
        ("dy_recv", (ny, 8, B), F32),
        ("roots", (ns, 8, B), F32),
        ("src1", (ns, B, width1), BF16),
        ("src2", (ns, B, width2), BF16),
    ]
    for layer, width in ((1, width1), (2, width2)):
        for chain, (n1, n2) in (("a", (ny, nx)), ("b", (nx, ny))):
            for way, steps in ((0, n1 // 2), (1, (n1 - 1) // 2)):
                for end in ("send", "recv"):
                    rows.append((f"{chain}1{way}{layer}{end}", (max(steps, 1), n2, H, width), BF16))
            for way, steps in ((0, n2 // 2), (1, (n2 - 1) // 2)):
                for end in ("send", "recv"):
                    rows.append((f"{chain}2{way}{layer}{end}", (max(steps, 1), H, width), BF16))
    return rows


class Links:
    def __init__(self, send_sems, recv_sems):
        self.send_sems, self.recv_sems = send_sems, recv_sems
        self.count = 0
        self.sent = []

    def make(self, src, dst, device):
        number = self.count
        self.count += 1
        made = pltpu.make_async_remote_copy(
            src_ref=src,
            dst_ref=dst,
            send_sem=self.send_sems.at[number],
            recv_sem=self.recv_sems.at[number],
            device_id=device,
            device_id_type=MESH,
        )
        self.sent.append(made)
        return made

    def copy(self, src, dst, device):
        made = self.make(src, dst, device)
        made.start()
        return made

    def finish(self):
        for made in self.sent:
            made.wait_send()


def order(slot, live, nb, count):
    lane = lax.broadcasted_iota(jnp.int32, (B, B), 1)
    sub = lax.broadcasted_iota(jnp.int32, (B, B), 0)
    value = jnp.broadcast_to(jnp.where(live > 0, slot, nb), (B, B))
    value_t = value.T
    key, key_t = value * count + lane, value_t * count + sub
    rank = jnp.sum((key_t < key).astype(jnp.int32), axis=0, keepdims=True)
    chosen = (jnp.broadcast_to(rank, (B, B)).T == lane).astype(jnp.int32)
    rows = [
        jnp.sum(chosen * sub, axis=0, keepdims=True),
        jnp.sum(chosen * value_t, axis=0, keepdims=True),
    ]
    for j in range(-(-nb // B)):
        block = lane + j * B
        upto = jnp.sum((value_t <= block).astype(jnp.int32), axis=0, keepdims=True)
        below = jnp.sum((value_t < block).astype(jnp.int32), axis=0, keepdims=True)
        rows.append(jnp.where(upto > below, upto - 1, count))
    while len(rows) < 8:
        rows.append(jnp.zeros((1, B), jnp.int32))
    return value, jnp.concatenate(rows, axis=0)


def kernel(dims, names, feat, adj, slot, live, w1, w2, out, *scratch):
    nx, ny, nz = dims
    nt, ns = nx * ny, 2 * nz
    nb = nt * ns
    count = adj.shape[0]
    buf = dict(zip(names, scratch))
    (tiles, sums, rowsum, dense, acc, ready1, scaled1, index_v, index_s, load_sems, index_sem, send_sems, recv_sems) = scratch[len(names):]
    links = Links(send_sems, recv_sems)

    me_s, me_t = lax.axis_index("src"), lax.axis_index("tgt")
    y, x = me_s // nx, lax.rem(me_s, nx)
    z, core = me_t // 2, lax.rem(me_t, 2)
    sign = 1 - 2 * core

    def at_x(d):
        return {"src": y * nx + wrap(x + d, nx)}

    def at_y(d):
        return {"src": wrap(y + d, ny) * nx + x}

    def at_z(d):
        return {"tgt": wrap(z + d, nz) * 2 + core}

    sibling = {"tgt": z * 2 + 1 - core}

    per_load = count // LOADS
    loads = []
    for j in range(LOADS):
        part = pl.ds(j * per_load, per_load)
        loads.append(pltpu.make_async_copy(adj.at[part], tiles.at[part], load_sems.at[j]))
        loads[-1].start()
    barrier = pltpu.get_barrier_semaphore()
    greeted = 0
    for d in range(1, nx):
        pl.semaphore_signal(barrier, inc=1, device_id=at_x(d), device_id_type=MESH)
        greeted += 1
    for d in range(1, ny):
        pl.semaphore_signal(barrier, inc=1, device_id=at_y(d), device_id_type=MESH)
        greeted += 1
    for d in range(1, ns):
        pl.semaphore_signal(
            barrier, inc=1, device_id={"tgt": lax.rem(me_t + d, ns)}, device_id_type=MESH
        )
        greeted += 1

    value, found = order(slot[...], live[...], nb, count)
    index_v[...] = found
    to_smem = pltpu.make_async_copy(index_v, index_s, index_sem)
    to_smem.start()

    buf["src1"][me_t] = feat[...]
    pl.semaphore_wait(barrier, greeted)

    def gather_start(ref, first, size):
        part = pl.ds(first, size)
        state = {"ref": ref, "part": part, "long": [], "short": [], "sibling": []}
        mine = ref.at[me_t, part]
        state["sibling"].append(links.copy(mine, mine, sibling))
        if nz > 1:
            state["long"].append(links.copy(mine, mine, at_z(sign)))
        if (nz - 1) // 2:
            state["short"].append(links.copy(mine, mine, at_z(-sign)))
        return state

    def gather_step(state, k):
        ref = state["ref"]
        for way, steps, d in (("long", nz // 2, sign), ("short", (nz - 1) // 2, -sign)):
            if k < steps:
                state[way][k].wait_recv()
                got = ref.at[wrap(z - d * (k + 1), nz) * 2 + core, state["part"]]
                if k + 1 < steps:
                    state[way].append(links.copy(got, got, at_z(d)))
                state["sibling"].append(links.copy(got, got, sibling))

    def gather_finish(state):
        for made in state["sibling"]:
            made.wait_recv()

    gathered = gather_start(buf["src1"], 0, B)

    ones = jnp.ones((8, B), BF16)
    group = min(16, per_load)
    for j in range(LOADS):
        loads[j].wait()

        def sum_rows(i, carry, j=j):
            first = j * per_load + i * group
            part = tiles[pl.ds(first, group)].reshape(group * B, B)
            got = lax.dot_general(ones, part, (((1,), (1,)), ((), ())), preferred_element_type=F32)
            for q in range(group):
                rowsum[first // group, q : q + 1, :] = got[0:1, q * B : (q + 1) * B]
            return carry

        lax.fori_loop(0, per_load // group, sum_rows, 0)
    row = lax.broadcasted_iota(jnp.int32, (nt, B), 0)
    target = lax.rem(row, ny) * nx + row // ny
    value_row = value[0:1]
    mine = (value_row >= target * ns) & (value_row < (target + 1) * ns)
    degree = jnp.dot(
        mine.astype(F32),
        rowsum[...].reshape(count, B),
        preferred_element_type=F32,
        precision=lax.Precision.HIGHEST,
    )
    for i in range(nx):
        buf["dx_send"][i] = degree[i * ny : (i + 1) * ny]
    dx = [
        links.copy(buf["dx_send"].at[wrap(x + d, nx)], buf["dx_recv"].at[d], at_x(d))
        for d in range(1, nx)
    ]

    to_smem.wait()
    sums[count] = jnp.zeros((B, B), BF16)

    def add_tile(i, carry):
        before, total = carry
        now = index_s[1, i]
        same = jnp.where(now == before, 1.0, 0.0).astype(F32)
        total = tiles[jnp.clip(index_s[0, i], 0, count - 1)].astype(F32) + total * same
        sums[i] = total.astype(BF16)
        return now, total

    lax.fori_loop(0, count, add_tile, (jnp.int32(-1), jnp.zeros((B, B), F32)), unroll=2)

    for made in dx:
        made.wait_recv()
    part = buf["dx_send"][x]
    for d in range(1, nx):
        part = part + buf["dx_recv"][d]
    for i in range(ny):
        buf["dy_send"][i] = jnp.broadcast_to(part[i : i + 1], (8, B))
    dy = [
        links.copy(buf["dy_send"].at[wrap(y + d, ny)], buf["dy_recv"].at[d], at_y(d))
        for d in range(1, ny)
    ]
    gather_step(gathered, 0)

    halves = ny // nx

    def distance(i, n):
        h, short = i // 2, lax.rem(i, 2)
        return sign * ((n // 2 - h) * (1 - short) - ((n - 1) // 2 - h) * short)

    def place(u, carry):
        i, r = u // nx, lax.rem(u, nx)
        t_a = wrap(y + distance(i, ny), ny) * nx + r
        t_b = (lax.rem(i, halves) * nx + r) * nx + wrap(x + distance(i // halves, nx), nx)
        for c in range(ns):
            for part, t in enumerate((t_a, t_b)):
                v = t * ns + c
                found = jnp.clip(index_s[2 + v // B, lax.rem(v, B)], 0, count)
                dense[i, part, r, :, c * B : (c + 1) * B] = sums[found, part * H : (part + 1) * H]
        return carry

    lax.fori_loop(0, nt // 2, place, 0)
    for made in dy:
        made.wait_recv()
    total = buf["dy_send"][y] + 1.0
    for d in range(1, ny):
        total = total + buf["dy_recv"][d]
    root = lax.rsqrt(total)
    buf["roots"][me_t] = root
    exchanged = [
        links.copy(
            buf["roots"].at[me_t], buf["roots"].at[me_t], {"tgt": lax.rem(me_t + d, ns)}
        )
        for d in range(1, ns)
    ]
    gather_step(gathered, 1)
    lax.fori_loop(nt // 2, nt, place, 0)
    for k in range(2, nz // 2):
        gather_step(gathered, k)
    own_root = jnp.broadcast_to(root[0:1], (B, B)).T
    scaled1[...] = (own_root * feat[...].astype(F32)).astype(BF16)
    gather_finish(gathered)
    for made in exchanged:
        made.wait_recv()
    roots_t = buf["roots"][...].reshape(ns * 8, B).T
    for c in range(ns):
        ready1[c] = (roots_t[:, 8 * c : 8 * c + 1] * buf["src1"][c].astype(F32)).astype(BF16)

    def spread(layer, width):
        source = ready1 if layer == 1 else buf["src2"]
        class Chain:
            def __init__(self, name, part, n1, n2, p1, p2, at1, at2):
                self.name, self.part = name, part
                self.n1, self.n2, self.p1, self.p2, self.at1, self.at2 = n1, n2, p1, p2, at1, at2
                self.steps1 = (n1 // 2, (n1 - 1) // 2)
                self.steps2 = (n2 // 2, (n2 - 1) // 2)
                self.made1, self.made2 = ({}, {}), ({}, {})
                self.size = 2 if n2 % 2 == 0 else 1
                self.subs = n2 // self.size

            def refs(self, phase, way):
                key = f"{self.name}{phase}{way}{layer}"
                return buf[key + "send"], buf[key + "recv"]

            def term(self, place, first, size):
                if self.part == 0:
                    return acc.at[place, 0, pl.ds(first, size), :, 0:width]
                lead = place * halves + first // nx
                return acc.at[lead, 1, pl.ds(lax.rem(first, nx), size), :, 0:width]

            def first(self, way):
                if not self.steps1[way]:
                    return
                send, recv = self.refs(1, way)
                for j in range(self.subs):
                    at = pl.ds(j * self.size, self.size)
                    self.made1[way][0, j] = links.make(
                        send.at[0, at], recv.at[0, at], self.at1(sign if way == 0 else -sign)
                    )

            def start_first(self, way):
                if not self.steps1[way]:
                    return
                send = self.refs(1, way)[0]
                for j in range(self.subs):
                    at = pl.ds(j * self.size, self.size)
                    send[0, at] = self.term(way, j * self.size, self.size)[...].astype(BF16)
                    self.made1[way][0, j].start()

            def send1(self, way, k, j):
                d = sign if way == 0 else -sign
                send, recv = self.refs(1, way)
                at = pl.ds(j * self.size, self.size)
                value = self.term(2 * k + way, j * self.size, self.size)[...]
                self.made1[way][k - 1, j].wait_recv()
                send[k, at] = (value + recv[k - 1, at].astype(F32)).astype(BF16)
                self.made1[way][k, j] = links.copy(send.at[k, at], recv.at[k, at], self.at1(d))

            def middle(self, j):
                at = pl.ds(j * self.size, self.size)
                term = self.term(self.n1 - 1, j * self.size, self.size)
                value = term[...]
                for way, steps in enumerate(self.steps1):
                    if steps:
                        self.made1[way][steps - 1, j].wait_recv()
                        value = value + self.refs(1, way)[1][steps - 1, at].astype(F32)
                term[...] = value

            def send2(self, way, k):
                d = sign if way == 0 else -sign
                send, recv = self.refs(2, way)
                place = wrap(self.p2 + d * (self.steps2[way] - k), self.n2)
                value = self.term(self.n1 - 1, place, 1)[...][0]
                if k:
                    self.made2[way][k - 1].wait_recv()
                    value = value + recv[k - 1].astype(F32)
                send[k] = value.astype(BF16)
                self.made2[way][k] = links.copy(send.at[k], recv.at[k], self.at2(d))

            def end(self):
                value = self.term(self.n1 - 1, self.p2, 1)[...][0]
                for way, steps in enumerate(self.steps2):
                    if steps:
                        self.made2[way][steps - 1].wait_recv()
                        value = value + self.refs(2, way)[1][steps - 1].astype(F32)
                return value

            def events(self, unit, shift):
                found = []
                for way, steps in enumerate(self.steps1):
                    for k in range(1, steps):
                        for j in range(self.subs):
                            at = (k - 1) * unit + unit * (j + 1) / self.subs
                            found.append((at + shift + 0.1 * way, functools.partial(self.send1, way, k, j)))
                last = max(self.steps1) * unit
                for j in range(self.subs):
                    found.append((last - unit + unit * (j + 1) / self.subs + shift, functools.partial(self.middle, j)))
                for way, steps in enumerate(self.steps2):
                    for k in range(steps):
                        at = last + 0.01 + 0.8 * k
                        found.append((at + shift + 0.1 * way, functools.partial(self.send2, way, k)))
                return found

        a = Chain("a", 0, ny, nx, y, x, at_y, at_x)
        b = Chain("b", 1, nx, ny, x, y, at_x, at_y)
        for way in range(2):
            a.first(way)
            b.first(way)

        def multiply(i, carry):
            right = source[...].reshape(ns * B, width)
            for part in range(2):
                left = dense[i, part].reshape(nx * H, ns * B)
                got = jnp.dot(left, right, preferred_element_type=F32)
                acc[i, part, :, :, 0:width] = got.reshape(nx, H, width)
            for way in range(2):
                pl.when(i == way)(functools.partial(a.start_first, way))
                pl.when(i == (way + 1) * halves - 1)(functools.partial(b.start_first, way))
            return carry

        lax.fori_loop(0, ny, multiply, 0)
        events = a.events(1.0, 0.0) + b.events(a.steps1[0] / max(b.steps1[0], 1), 0.05)
        for _, event in sorted(events, key=lambda entry: entry[0]):
            event()
        return a.end, b.end

    def finish_rows(end, first, scaled, weight):
        summed = end()
        root_b = jnp.concatenate([own_root[first : first + H]] * (summed.shape[1] // B), axis=1)
        combined = (root_b * (summed + scaled.astype(F32))).astype(BF16)
        got = jnp.dot(combined, weight[...], preferred_element_type=F32)
        return jnp.maximum(got, 0.0).astype(BF16)

    width1, width2 = feat.shape[1], w1.shape[1]
    gathers = []
    for half, end in enumerate(spread(1, width1)):
        rows = slice(half * H, (half + 1) * H)
        hidden = finish_rows(end, half * H, scaled1[rows], w1)
        root_2 = jnp.concatenate([own_root[rows]] * (width2 // B), axis=1)
        buf["src2"][me_t, rows] = (root_2 * hidden.astype(F32)).astype(BF16)
        gathers.append(gather_start(buf["src2"], half * H, H))
    for k in range(nz // 2):
        for state in gathers:
            gather_step(state, k)
    for state in gathers:
        gather_finish(state)
    for half, end in enumerate(spread(2, width2)):
        rows = slice(half * H, (half + 1) * H)
        out[rows] = finish_rows(end, half * H, buf["src2"][me_t, rows], w2)
    links.finish()


def on_device(dims, features, adjacency, tile_slot, tile_live, first_weight, second_weight):
    nx, ny, nz = dims
    nt, ns = nx * ny, 2 * nz
    count = adjacency.shape[2]
    width1, width2 = first_weight.shape
    rows = plan(nx, ny, nz, width1, width2)
    copies = 300
    vmem = pl.BlockSpec(memory_space=pltpu.VMEM)
    group = min(16, count // LOADS)
    return pl.pallas_call(
        functools.partial(kernel, dims, [name for name, _, _ in rows]),
        out_shape=jax.ShapeDtypeStruct((B, second_weight.shape[1]), BF16),
        in_specs=[vmem, pl.BlockSpec(memory_space=pl.ANY), vmem, vmem, vmem, vmem],
        out_specs=vmem,
        scratch_shapes=[pltpu.VMEM(shape, dtype) for _, shape, dtype in rows]
        + [
            pltpu.VMEM((count, B, B), BF16),
            pltpu.VMEM((count + 1, B, B), BF16),
            pltpu.VMEM((count // group, group, B), F32),
            pltpu.VMEM((ny, 2, nx, H, ns * B), BF16),
            pltpu.VMEM((ny, 2, nx, H, width2), F32),
            pltpu.VMEM((ns, B, width1), BF16),
            pltpu.VMEM((B, width1), BF16),
            pltpu.VMEM((8, B), jnp.int32),
            pltpu.SMEM((8, B), jnp.int32),
            pltpu.SemaphoreType.DMA((LOADS,)),
            pltpu.SemaphoreType.DMA,
            pltpu.SemaphoreType.DMA((copies,)),
            pltpu.SemaphoreType.DMA((copies,)),
        ],
        compiler_params=pltpu.CompilerParams(
            collective_id=0, has_side_effects=True, vmem_limit_bytes=56 * 2**20
        ),
    )(
        features,
        adjacency[0, 0],
        tile_slot[0],
        tile_live[0],
        first_weight,
        second_weight,
    )


def solution(mesh, nx=NX):
    dims = (nx, mesh.shape["src"] // nx, mesh.shape["tgt"] // 2)
    placed = (
        P(("tgt", "src"), None),
        P("tgt", "src", None, None, None),
        P("tgt", "src", None),
        P("tgt", "src", None),
        P(),
        P(),
    )
    return jax.shard_map(
        functools.partial(on_device, dims),
        mesh=mesh,
        in_specs=placed,
        out_specs=P(("tgt", "src"), None),
        check_vma=False,
    )
```

```python
import functools

import jax
import jax.numpy as jnp
from jax import lax
from jax.experimental import pallas as pl
from jax.experimental.pallas import tpu as pltpu
from jax.sharding import PartitionSpec as P

MESH = pl.DeviceIdType.MESH
F32 = jnp.float32
BF16 = jnp.bfloat16
NX = 4
B = 128
H = B // 2
LOADS = 4


def wrap(a, n):
    return lax.rem(a + n, n)


def plan(nx, ny, nz, width1, width2):
    ns = 2 * nz
    rows = [
        ("dx_send", (nx, ny, B), F32),
        ("dx_recv", (nx, ny, B), F32),
        ("dy_send", (ny, 8, B), F32),
        ("dy_recv", (ny, 8, B), F32),
        ("roots", (ns, 8, B), F32),
        ("src1", (ns, B, width1), BF16),
        ("src2", (ns, B, width2), BF16),
    ]
    for layer, width in ((1, width1), (2, width2)):
        for chain, (n1, n2) in (("a", (ny, nx)), ("b", (nx, ny))):
            for way, steps in ((0, n1 // 2), (1, (n1 - 1) // 2)):
                for end in ("send", "recv"):
                    rows.append((f"{chain}1{way}{layer}{end}", (max(steps, 1), n2, H, width), BF16))
            for way, steps in ((0, n2 // 2), (1, (n2 - 1) // 2)):
                for end in ("send", "recv"):
                    rows.append((f"{chain}2{way}{layer}{end}", (max(steps, 1), H, width), BF16))
    return rows


class Links:
    def __init__(self, send_sems, recv_sems):
        self.send_sems, self.recv_sems = send_sems, recv_sems
        self.count = 0
        self.sent = []

    def make(self, src, dst, device):
        number = self.count
        self.count += 1
        made = pltpu.make_async_remote_copy(
            src_ref=src,
            dst_ref=dst,
            send_sem=self.send_sems.at[number],
            recv_sem=self.recv_sems.at[number],
            device_id=device,
            device_id_type=MESH,
        )
        self.sent.append(made)
        return made

    def copy(self, src, dst, device):
        made = self.make(src, dst, device)
        made.start()
        return made

    def finish(self):
        for made in self.sent:
            made.wait_send()


def order(slot, live, nb, count):
    lane = lax.broadcasted_iota(jnp.int32, (B, B), 1)
    sub = lax.broadcasted_iota(jnp.int32, (B, B), 0)
    value = jnp.broadcast_to(jnp.where(live > 0, slot, nb), (B, B))
    value_t = value.T
    key, key_t = value * count + lane, value_t * count + sub
    rank = jnp.sum((key_t < key).astype(jnp.int32), axis=0, keepdims=True)
    chosen = (jnp.broadcast_to(rank, (B, B)).T == lane).astype(jnp.int32)
    rows = [
        jnp.sum(chosen * sub, axis=0, keepdims=True),
        jnp.sum(chosen * value_t, axis=0, keepdims=True),
    ]
    for j in range(-(-nb // B)):
        block = lane + j * B
        upto = jnp.sum((value_t <= block).astype(jnp.int32), axis=0, keepdims=True)
        below = jnp.sum((value_t < block).astype(jnp.int32), axis=0, keepdims=True)
        rows.append(jnp.where(upto > below, upto - 1, count))
    while len(rows) < 8:
        rows.append(jnp.zeros((1, B), jnp.int32))
    return value, jnp.concatenate(rows, axis=0)


def kernel(dims, names, feat, adj, slot, live, w1, w2, out, *scratch):
    nx, ny, nz = dims
    nt, ns = nx * ny, 2 * nz
    nb = nt * ns
    count = adj.shape[0]
    buf = dict(zip(names, scratch))
    (tiles, sums, rowsum, dense, acc, ready1, scaled1, index_v, index_s, load_sems, index_sem, send_sems, recv_sems) = scratch[len(names):]
    links = Links(send_sems, recv_sems)

    me_s, me_t = lax.axis_index("src"), lax.axis_index("tgt")
    y, x = me_s // nx, lax.rem(me_s, nx)
    z, core = me_t // 2, lax.rem(me_t, 2)
    sign = 1 - 2 * core

    def at_x(d):
        return {"src": y * nx + wrap(x + d, nx)}

    def at_y(d):
        return {"src": wrap(y + d, ny) * nx + x}

    def at_z(d):
        return {"tgt": wrap(z + d, nz) * 2 + core}

    sibling = {"tgt": z * 2 + 1 - core}

    per_load = count // LOADS
    loads = []
    for j in range(LOADS):
        part = pl.ds(j * per_load, per_load)
        loads.append(pltpu.make_async_copy(adj.at[part], tiles.at[part], load_sems.at[j]))
        loads[-1].start()
    barrier = pltpu.get_barrier_semaphore()
    greeted = 0
    for d in range(1, nx):
        pl.semaphore_signal(barrier, inc=1, device_id=at_x(d), device_id_type=MESH)
        greeted += 1
    for d in range(1, ny):
        pl.semaphore_signal(barrier, inc=1, device_id=at_y(d), device_id_type=MESH)
        greeted += 1
    for d in range(1, ns):
        pl.semaphore_signal(
            barrier, inc=1, device_id={"tgt": lax.rem(me_t + d, ns)}, device_id_type=MESH
        )
        greeted += 1

    value, found = order(slot[...], live[...], nb, count)
    index_v[...] = found
    to_smem = pltpu.make_async_copy(index_v, index_s, index_sem)
    to_smem.start()

    buf["src1"][me_t] = feat[...]
    pl.semaphore_wait(barrier, greeted)

    def gather_start(ref, first, size):
        part = pl.ds(first, size)
        state = {"ref": ref, "part": part, "long": [], "short": [], "sibling": []}
        mine = ref.at[me_t, part]
        state["sibling"].append(links.copy(mine, mine, sibling))
        if nz > 1:
            state["long"].append(links.copy(mine, mine, at_z(sign)))
        if (nz - 1) // 2:
            state["short"].append(links.copy(mine, mine, at_z(-sign)))
        return state

    def gather_step(state, k):
        ref = state["ref"]
        for way, steps, d in (("long", nz // 2, sign), ("short", (nz - 1) // 2, -sign)):
            if k < steps:
                state[way][k].wait_recv()
                got = ref.at[wrap(z - d * (k + 1), nz) * 2 + core, state["part"]]
                if k + 1 < steps:
                    state[way].append(links.copy(got, got, at_z(d)))
                state["sibling"].append(links.copy(got, got, sibling))

    def gather_finish(state):
        for made in state["sibling"]:
            made.wait_recv()

    gathered = gather_start(buf["src1"], 0, B)

    ones = jnp.ones((8, B), BF16)
    group = min(16, per_load)
    for j in range(LOADS):
        loads[j].wait()

        def sum_rows(i, carry, j=j):
            first = j * per_load + i * group
            part = tiles[pl.ds(first, group)].reshape(group * B, B)
            got = lax.dot_general(ones, part, (((1,), (1,)), ((), ())), preferred_element_type=F32)
            for q in range(group):
                rowsum[first // group, q : q + 1, :] = got[0:1, q * B : (q + 1) * B]
            return carry

        lax.fori_loop(0, per_load // group, sum_rows, 0)
    row = lax.broadcasted_iota(jnp.int32, (nt, B), 0)
    target = lax.rem(row, ny) * nx + row // ny
    value_row = value[0:1]
    mine = (value_row >= target * ns) & (value_row < (target + 1) * ns)
    degree = jnp.dot(
        mine.astype(F32),
        rowsum[...].reshape(count, B),
        preferred_element_type=F32,
        precision=lax.Precision.HIGHEST,
    )
    for i in range(nx):
        buf["dx_send"][i] = degree[i * ny : (i + 1) * ny]
    dx = [
        links.copy(buf["dx_send"].at[wrap(x + d, nx)], buf["dx_recv"].at[d], at_x(d))
        for d in range(1, nx)
    ]

    to_smem.wait()
    sums[count] = jnp.zeros((B, B), BF16)

    def add_tile(i, carry):
        before, total = carry
        now = index_s[1, i]
        same = jnp.where(now == before, 1.0, 0.0).astype(F32)
        total = tiles[jnp.clip(index_s[0, i], 0, count - 1)].astype(F32) + total * same
        sums[i] = total.astype(BF16)
        return now, total

    lax.fori_loop(0, count, add_tile, (jnp.int32(-1), jnp.zeros((B, B), F32)), unroll=2)

    for made in dx:
        made.wait_recv()
    part = buf["dx_send"][x]
    for d in range(1, nx):
        part = part + buf["dx_recv"][d]
    for i in range(ny):
        buf["dy_send"][i] = jnp.broadcast_to(part[i : i + 1], (8, B))
    dy = [
        links.copy(buf["dy_send"].at[wrap(y + d, ny)], buf["dy_recv"].at[d], at_y(d))
        for d in range(1, ny)
    ]
    gather_step(gathered, 0)

    halves = ny // nx

    def distance(i, n):
        h, short = i // 2, lax.rem(i, 2)
        return sign * ((n // 2 - h) * (1 - short) - ((n - 1) // 2 - h) * short)

    def place(u, carry):
        i, r = u // nx, lax.rem(u, nx)
        t_a = wrap(y + distance(i, ny), ny) * nx + r
        t_b = (lax.rem(i, halves) * nx + r) * nx + wrap(x + distance(i // halves, nx), nx)
        for c in range(ns):
            for part, t in enumerate((t_a, t_b)):
                v = t * ns + c
                found = jnp.clip(index_s[2 + v // B, lax.rem(v, B)], 0, count)
                dense[i, part, r, :, c * B : (c + 1) * B] = sums[found, part * H : (part + 1) * H]
        return carry

    lax.fori_loop(0, nt // 2, place, 0)
    for made in dy:
        made.wait_recv()
    total = buf["dy_send"][y] + 1.0
    for d in range(1, ny):
        total = total + buf["dy_recv"][d]
    root = lax.rsqrt(total)
    buf["roots"][me_t] = root
    exchanged = [
        links.copy(
            buf["roots"].at[me_t], buf["roots"].at[me_t], {"tgt": lax.rem(me_t + d, ns)}
        )
        for d in range(1, ns)
    ]
    gather_step(gathered, 1)
    lax.fori_loop(nt // 2, nt, place, 0)
    for k in range(2, nz // 2):
        gather_step(gathered, k)
    own_root = jnp.broadcast_to(root[0:1], (B, B)).T
    scaled1[...] = (own_root * feat[...].astype(F32)).astype(BF16)
    gather_finish(gathered)
    for made in exchanged:
        made.wait_recv()
    roots_t = buf["roots"][...].reshape(ns * 8, B).T
    for c in range(ns):
        ready1[c] = (roots_t[:, 8 * c : 8 * c + 1] * buf["src1"][c].astype(F32)).astype(BF16)

    def spread(layer, width):
        source = ready1 if layer == 1 else buf["src2"]
        class Chain:
            def __init__(self, name, part, n1, n2, p1, p2, at1, at2):
                self.name, self.part = name, part
                self.n1, self.n2, self.p1, self.p2, self.at1, self.at2 = n1, n2, p1, p2, at1, at2
                self.steps1 = (n1 // 2, (n1 - 1) // 2)
                self.steps2 = (n2 // 2, (n2 - 1) // 2)
                self.made1, self.made2 = ({}, {}), ({}, {})
                self.size = 4 if n2 % 4 == 0 else 1
                self.subs = n2 // self.size

            def refs(self, phase, way):
                key = f"{self.name}{phase}{way}{layer}"
                return buf[key + "send"], buf[key + "recv"]

            def term(self, place, first, size):
                if self.part == 0:
                    return acc.at[place, 0, pl.ds(first, size), :, 0:width]
                lead = place * halves + first // nx
                return acc.at[lead, 1, pl.ds(lax.rem(first, nx), size), :, 0:width]

            def first(self, way):
                if not self.steps1[way]:
                    return
                send, recv = self.refs(1, way)
                for j in range(self.subs):
                    at = pl.ds(j * self.size, self.size)
                    self.made1[way][0, j] = links.make(
                        send.at[0, at], recv.at[0, at], self.at1(sign if way == 0 else -sign)
                    )

            def start_first(self, way):
                if not self.steps1[way]:
                    return
                send = self.refs(1, way)[0]
                for j in range(self.subs):
                    at = pl.ds(j * self.size, self.size)
                    send[0, at] = self.term(way, j * self.size, self.size)[...].astype(BF16)
                    self.made1[way][0, j].start()

            def send1(self, way, k, j):
                d = sign if way == 0 else -sign
                send, recv = self.refs(1, way)
                at = pl.ds(j * self.size, self.size)
                value = self.term(2 * k + way, j * self.size, self.size)[...]
                self.made1[way][k - 1, j].wait_recv()
                send[k, at] = (value + recv[k - 1, at].astype(F32)).astype(BF16)
                self.made1[way][k, j] = links.copy(send.at[k, at], recv.at[k, at], self.at1(d))

            def middle(self, j):
                at = pl.ds(j * self.size, self.size)
                term = self.term(self.n1 - 1, j * self.size, self.size)
                value = term[...]
                for way, steps in enumerate(self.steps1):
                    if steps:
                        self.made1[way][steps - 1, j].wait_recv()
                        value = value + self.refs(1, way)[1][steps - 1, at].astype(F32)
                term[...] = value

            def send2(self, way, k):
                d = sign if way == 0 else -sign
                send, recv = self.refs(2, way)
                place = wrap(self.p2 + d * (self.steps2[way] - k), self.n2)
                value = self.term(self.n1 - 1, place, 1)[...][0]
                if k:
                    self.made2[way][k - 1].wait_recv()
                    value = value + recv[k - 1].astype(F32)
                send[k] = value.astype(BF16)
                self.made2[way][k] = links.copy(send.at[k], recv.at[k], self.at2(d))

            def end(self):
                value = self.term(self.n1 - 1, self.p2, 1)[...][0]
                for way, steps in enumerate(self.steps2):
                    if steps:
                        self.made2[way][steps - 1].wait_recv()
                        value = value + self.refs(2, way)[1][steps - 1].astype(F32)
                return value

            def events(self, unit, shift):
                found = []
                for way, steps in enumerate(self.steps1):
                    for k in range(1, steps):
                        for j in range(self.subs):
                            at = (k - 1) * unit + unit * (j + 1) / self.subs
                            found.append((at + shift + 0.1 * way, functools.partial(self.send1, way, k, j)))
                last = max(self.steps1) * unit
                for j in range(self.subs):
                    found.append((last - unit + unit * (j + 1) / self.subs + shift, functools.partial(self.middle, j)))
                for way, steps in enumerate(self.steps2):
                    for k in range(steps):
                        at = last + 0.01 + 0.8 * k
                        found.append((at + shift + 0.1 * way, functools.partial(self.send2, way, k)))
                return found

        a = Chain("a", 0, ny, nx, y, x, at_y, at_x)
        b = Chain("b", 1, nx, ny, x, y, at_x, at_y)
        for way in range(2):
            a.first(way)
            b.first(way)

        def multiply(i, carry):
            right = source[...].reshape(ns * B, width)
            for part in range(2):
                left = dense[i, part].reshape(nx * H, ns * B)
                got = jnp.dot(left, right, preferred_element_type=F32)
                acc[i, part, :, :, 0:width] = got.reshape(nx, H, width)
            for way in range(2):
                pl.when(i == way)(functools.partial(a.start_first, way))
                pl.when(i == (way + 1) * halves - 1)(functools.partial(b.start_first, way))
            return carry

        lax.fori_loop(0, ny, multiply, 0)
        events = a.events(1.0, 0.0) + b.events(a.steps1[0] / max(b.steps1[0], 1), 0.05)
        for _, event in sorted(events, key=lambda entry: entry[0]):
            event()
        return a.end, b.end

    def finish_rows(end, first, scaled, weight):
        summed = end()
        root_b = jnp.concatenate([own_root[first : first + H]] * (summed.shape[1] // B), axis=1)
        combined = (root_b * (summed + scaled.astype(F32))).astype(BF16)
        got = jnp.dot(combined, weight[...], preferred_element_type=F32)
        return jnp.maximum(got, 0.0).astype(BF16)

    width1, width2 = feat.shape[1], w1.shape[1]
    gathers = []
    for half, end in enumerate(spread(1, width1)):
        rows = slice(half * H, (half + 1) * H)
        hidden = finish_rows(end, half * H, scaled1[rows], w1)
        root_2 = jnp.concatenate([own_root[rows]] * (width2 // B), axis=1)
        buf["src2"][me_t, rows] = (root_2 * hidden.astype(F32)).astype(BF16)
        gathers.append(gather_start(buf["src2"], half * H, H))
    for k in range(nz // 2):
        for state in gathers:
            gather_step(state, k)
    for state in gathers:
        gather_finish(state)
    for half, end in enumerate(spread(2, width2)):
        rows = slice(half * H, (half + 1) * H)
        out[rows] = finish_rows(end, half * H, buf["src2"][me_t, rows], w2)
    links.finish()


def on_device(dims, features, adjacency, tile_slot, tile_live, first_weight, second_weight):
    nx, ny, nz = dims
    nt, ns = nx * ny, 2 * nz
    count = adjacency.shape[2]
    width1, width2 = first_weight.shape
    rows = plan(nx, ny, nz, width1, width2)
    copies = 300
    vmem = pl.BlockSpec(memory_space=pltpu.VMEM)
    group = min(16, count // LOADS)
    return pl.pallas_call(
        functools.partial(kernel, dims, [name for name, _, _ in rows]),
        out_shape=jax.ShapeDtypeStruct((B, second_weight.shape[1]), BF16),
        in_specs=[vmem, pl.BlockSpec(memory_space=pl.ANY), vmem, vmem, vmem, vmem],
        out_specs=vmem,
        scratch_shapes=[pltpu.VMEM(shape, dtype) for _, shape, dtype in rows]
        + [
            pltpu.VMEM((count, B, B), BF16),
            pltpu.VMEM((count + 1, B, B), BF16),
            pltpu.VMEM((count // group, group, B), F32),
            pltpu.VMEM((ny, 2, nx, H, ns * B), BF16),
            pltpu.VMEM((ny, 2, nx, H, width2), F32),
            pltpu.VMEM((ns, B, width1), BF16),
            pltpu.VMEM((B, width1), BF16),
            pltpu.VMEM((8, B), jnp.int32),
            pltpu.SMEM((8, B), jnp.int32),
            pltpu.SemaphoreType.DMA((LOADS,)),
            pltpu.SemaphoreType.DMA,
            pltpu.SemaphoreType.DMA((copies,)),
            pltpu.SemaphoreType.DMA((copies,)),
        ],
        compiler_params=pltpu.CompilerParams(
            collective_id=0, has_side_effects=True, vmem_limit_bytes=56 * 2**20
        ),
    )(
        features,
        adjacency[0, 0],
        tile_slot[0],
        tile_live[0],
        first_weight,
        second_weight,
    )


def solution(mesh, nx=NX):
    dims = (nx, mesh.shape["src"] // nx, mesh.shape["tgt"] // 2)
    placed = (
        P(("tgt", "src"), None),
        P("tgt", "src", None, None, None),
        P("tgt", "src", None),
        P("tgt", "src", None),
        P(),
        P(),
    )
    return jax.shard_map(
        functools.partial(on_device, dims),
        mesh=mesh,
        in_specs=placed,
        out_specs=P(("tgt", "src"), None),
        check_vma=False,
    )
```
